32 devices in a mesh: dp: 8 (over y, x, core), tensor: 4 (over z).
Axes of the slice: x: 2, y: 2, z: 4, core: 2. Of those that a mesh axis runs over, the one named last changes fastest.
Arguments:
- inputs: bfloat16 [4096, 6144], P(('dp', 'tensor')), may hold values from -36 to 36
- gain: float32 [6144], replicated, may hold values from 0.25 to 1.75
- w_in: bfloat16 [6144, 12288], P(None, 'tensor'), may hold values from -0.078125 to 0.078125
- grad_act: bfloat16 [4096, 12288], P('dp', 'tensor'), may hold values from -6 to 6
- residual_gradient: bfloat16 [4096, 6144], P(('dp', 'tensor')), may hold values from -6 to 6
Outputs:
- block_input_gradient: bfloat16 [4096, 6144], P(('dp', 'tensor'))
- grad_w: float32 [6144, 12288], P('dp', 'tensor')
- scale_gradient: float32 [6144], replicated
The draws below stay inside these ranges and needn't reach their ends.
All inputs are finite; a program needn't handle non-finite values.
Results may differ from the reference program's by a relative error of at most 0.022.
Values may be sent and summed in bfloat16 or wider, within the bound.
A program may use at most 192 MiB of HBM per device.

```python
import math
import jax
import jax.numpy as jnp
from jax import lax

D = 6144
FF = 12288
TOK = 512
TOKENS = 4096
N_DP = 8
N_TENSOR = 4


def draw_inputs(key, part):
    keys = jax.random.split(key, 3)
    row_scale = jnp.exp(jax.random.uniform(keys[0], (TOKENS, 1), jnp.float32, math.log(0.3), math.log(3.0)))
    col_scale = jnp.exp(jax.random.uniform(keys[1], (1, D), jnp.float32, math.log(0.3), math.log(3.0)))
    base = jax.random.truncated_normal(keys[2], -4.0, 4.0, (TOKENS, D), jnp.float32)
    values = row_scale * col_scale * base
    return jnp.clip(values, -36.0, 36.0).astype(jnp.bfloat16)


def level_of(own_key, shape, cuts, smallest, top_value):
    level, own = 1.0, jax.random.fold_in(own_key, 6)
    for axis_at, parts in cuts:
        steps = jnp.exp(jax.random.uniform(jax.random.fold_in(own, axis_at), (parts,), jnp.float32, smallest / len(cuts), top_value / len(cuts)))
        level = level * jnp.repeat(steps, shape[axis_at] // parts).reshape([-1 if axis == axis_at else 1 for axis in range(len(shape))])
    return level


def centred(stream_key, shape, deviation, limit, cuts=(), kind=jnp.bfloat16):
    result = deviation * jax.random.normal(stream_key, shape, jnp.float32)
    if cuts:
        result = result * level_of(stream_key, shape, cuts, -0.22, 0.18)
    return jnp.clip(result, -limit, limit).astype(kind)


def setup_inputs(seed: int = 0) -> dict:
    seeds = jax.random.split(jax.random.key(seed), 6)
    inputs = draw_inputs(jax.random.fold_in(seeds[5], 71), 0)
    gain = jnp.clip(1.0 + 0.15 * jax.random.normal(seeds[1], (D,), jnp.float32), 0.25, 1.75)
    w_in = centred(seeds[2], (D, FF), D ** -0.5, 0.078125, ((1, 4),))
    grad_act = centred(seeds[3], (TOKENS, FF), 1.0, 6.0, ((0, 8), (1, 4)))
    residual_gradient = centred(seeds[4], (TOKENS, D), 1.0, 6.0, ((0, 32),))
    return dict(inputs=inputs, gain=gain, w_in=w_in, grad_act=grad_act, residual_gradient=residual_gradient)


def reference(inputs, gain, w_in, grad_act, residual_gradient):
    values = inputs.astype(jnp.float32)
    centered_input = values - lax.optimization_barrier(jnp.mean(values, axis=1, keepdims=True))
    inverse_deviation = lax.rsqrt(lax.optimization_barrier(jnp.mean(centered_input * centered_input, axis=1, keepdims=True)) + 1e-06)
    standardized_input = centered_input * inverse_deviation
    normed_output = (standardized_input * gain).astype(jnp.bfloat16)
    pre = jnp.dot(normed_output, w_in, preferred_element_type=jnp.float32)
    unused, pullback = jax.vjp(jax.nn.gelu, pre)
    dpre = pullback(grad_act.astype(jnp.float32))[0].astype(jnp.bfloat16)
    width = FF // N_TENSOR

    def add_block(total, index):
        start = (index * width).astype(jnp.int32)
        cols = lax.dynamic_slice_in_dim(dpre, start, width, 1)
        rows = lax.dynamic_slice_in_dim(w_in, start, width, 1)
        part = lax.dot_general(cols, rows, (((1,), (1,)), ((), ())), preferred_element_type=jnp.float32)
        return (total + lax.optimization_barrier(part.astype(jnp.bfloat16)).astype(jnp.float32), None)
    normed_gradient, unused_b = lax.scan(add_block, jnp.zeros((TOKENS, D), jnp.float32), jnp.arange(N_TENSOR, dtype=jnp.int32))
    scale_gradient = lax.optimization_barrier(jnp.sum(normed_gradient * standardized_input, axis=0)) / N_DP
    scaled_gradient = normed_gradient * gain
    first_average = lax.optimization_barrier(jnp.mean(scaled_gradient, axis=1, keepdims=True))
    second_average = lax.optimization_barrier(jnp.mean(scaled_gradient * standardized_input, axis=1, keepdims=True))
    block_input_gradient = (residual_gradient.astype(jnp.float32) + inverse_deviation * (scaled_gradient - first_average - standardized_input * second_average)).astype(jnp.bfloat16)

    def add_replica(total, index):
        start = (index * TOK).astype(jnp.int32)
        left = lax.dynamic_slice_in_dim(normed_output, start, TOK, 0)
        right = lax.dynamic_slice_in_dim(dpre, start, TOK, 0)
        part = lax.dot_general(left, right, (((0,), (0,)), ((), ())), preferred_element_type=jnp.float32)
        return (total + lax.optimization_barrier(part.astype(jnp.bfloat16)).astype(jnp.float32), None)
    summed, unused_c = lax.scan(add_replica, jnp.zeros((D, FF), jnp.float32), jnp.arange(N_DP, dtype=jnp.int32))
    grad_w = summed / N_DP
    return (block_input_gradient, grad_w, scale_gradient)
```

```python
import functools

import jax
import jax.numpy as jnp
from jax import lax
from jax.experimental import pallas as pl
from jax.experimental.pallas import tpu as pltpu
from jax.sharding import PartitionSpec as P

MESH = pl.DeviceIdType.MESH
STAGES = 2


def contract_rows(left, right):
    return lax.dot_general(
        left, right, (((0,), (0,)), ((), ())), preferred_element_type=jnp.float32
    )


def gelu_slope(v):
    c = 0.7978845608028654
    vv = v * v
    th = jnp.tanh(c * v * (1.0 + 0.044715 * vv))
    return 0.5 * (1.0 + th) + 0.5 * v * (1.0 - th * th) * (c * (1.0 + 0.134145 * vv))


def kernel(
    n_t, n_h, J, c,
    nrm, w, ga, ng, gd, gn,
    w_v, ag, part, rr, dp,
    ld_w, ld_ga, ld_n,
    ag_recv, ag_send_r, ag_send_l,
    xn_send, xn_recv, xd_send, xd_recv,
    rs_recv_r, rs_recv_l, rs_send_r, rs_send_l,
    cn, cd, cg,
):
    t = lax.axis_index("tensor")
    d = lax.axis_index("dp")
    hi, core = d // 2, lax.rem(d, 2)
    D, F = w_v.shape
    W = D // n_h
    last = n_t - 1

    def rows(s):
        return pl.ds(pl.multiple_of(s * c, c), c)

    def peer(p):
        return lax.rem(hi + p, n_h)

    def came_from(p):
        return lax.rem(hi - p + n_h, n_h)

    def step(right):
        return {"tensor": lax.rem(t + 1, n_t) if right else lax.rem(t + last, n_t)}

    def ag_copy(j, s, right):
        block = ag.at[j, rows(s), :]
        sems = ag_send_r if right else ag_send_l
        return pltpu.make_async_remote_copy(
            block, block, sems.at[j, s], ag_recv.at[j, s],
            device_id=step(right), device_id_type=MESH)

    def rs_copy(j, s, right):
        slot = s + 1 if right else s
        send, recv = (rs_send_r, rs_recv_l) if right else (rs_send_l, rs_recv_r)
        return pltpu.make_async_remote_copy(
            part.at[j, rows(s), :], rr.at[j, rows(slot), :], send.at[j, s], recv.at[j, s],
            device_id=step(right), device_id_type=MESH)

    def xn_copy(j, s, p, whose):
        cols = pl.ds(pl.multiple_of(peer(p) * W, W), W)
        return pltpu.make_async_remote_copy(
            ag.at[j, rows(s), cols], ng.at[whose, j, rows(s), :],
            xn_send.at[j, s, p], xn_recv.at[j, s, p],
            device_id={"dp": peer(p) * 2 + core}, device_id_type=MESH)

    def xd_copy(j, p, whose):
        return pltpu.make_async_remote_copy(
            dp.at[j], gd.at[whose, j], xd_send.at[j, p], xd_recv.at[j, p],
            device_id={"dp": peer(p) * 2 + core}, device_id_type=MESH)

    def own_cols(j):
        return pltpu.make_async_copy(
            ag.at[j, :, pl.ds(pl.multiple_of(hi * W, W), W)], ng.at[hi, j], cn.at[j])

    def own_dpre(j):
        return pltpu.make_async_copy(dp.at[j], gd.at[hi, j], cd.at[j])

    pieces = ld_w.shape[0]
    depth = D // pieces

    def w_copy(i):
        r = pl.ds(i * depth, depth)
        return pltpu.make_async_copy(w.at[r, :], w_v.at[r, :], ld_w.at[i])

    def n_copy(j):
        return pltpu.make_async_copy(nrm.at[j], ag.at[j, rows(t), :], ld_n.at[j])

    def ga_copy(j, s):
        return pltpu.make_async_copy(ga.at[s, j], dp.at[j, pl.ds(s * c, c), :], ld_ga.at[j, s])

    for j in range(J):
        n_copy(j).start()
    barrier = pltpu.get_barrier_semaphore()
    for right in (True, False):
        @pl.when(t < last if right else t > 0)
        def _():
            pl.semaphore_signal(barrier, inc=1, device_id=step(right), device_id_type=MESH)
    for p in range(1, n_h):
        pl.semaphore_signal(barrier, inc=1, device_id={"dp": peer(p) * 2 + core}, device_id_type=MESH)
    pl.semaphore_wait(barrier, n_h - 1 + jnp.minimum(t, 1) + jnp.minimum(last - t, 1))
    for j in range(J):
        n_copy(j).wait()

    def send_own(j, right):
        @pl.when(t < last if right else t > 0)
        def _():
            ag_copy(j, t, right).start()

    def spread(j, s):
        for p in range(1, n_h):
            xn_copy(j, s, p, hi).start()

    send_own(0, True)
    send_own(0, False)
    for i in range(pieces):
        w_copy(i).start()
    for j in range(J):
        for s in range(n_t):
            ga_copy(j, s).start()
    for j in range(J):
        spread(j, t)

    def next_own(j, k):
        if j + 1 < J:
            @pl.when(k == t)
            def _():
                send_own(j + 1, True)

            @pl.when(k == last - t)
            def _():
                send_own(j + 1, False)

    def ag_round(j, k):
        next_own(j, k)

        @pl.when(k < t)
        def _():
            s = t - 1 - k
            ag_copy(j, s, True).wait_recv()

            @pl.when(t < last)
            def _():
                ag_copy(j, s, True).start()
            spread(j, s)

        @pl.when(k < last - t)
        def _():
            s = t + 1 + k
            ag_copy(j, s, False).wait_recv()

            @pl.when(t > 0)
            def _():
                ag_copy(j, s, False).start()
            spread(j, s)

    def make_dpre(j):
        ft = 512 if F % 512 == 0 else 256

        def tile(i, _):
            cols = pl.ds(pl.multiple_of(i * ft, ft), ft)
            pre = jnp.dot(ag[j], w_v[:, cols], preferred_element_type=jnp.float32)
            g = dp[j, :, cols].astype(jnp.float32)
            dp[j, :, cols] = (g * gelu_slope(pre)).astype(jnp.bfloat16)
            return 0
        lax.fori_loop(0, F // ft, tile, 0)
        for p in range(1, n_h):
            xd_copy(j, p, hi).start()
        own_dpre(j).start()

    def make_parts(j):
        dt = 256

        def tile(i, _):
            cols = pl.ds(pl.multiple_of(i * dt, dt), dt)
            part[j, :, cols] = lax.dot_general(
                dp[j], w_v[cols, :], (((1,), (1,)), ((), ())),
                preferred_element_type=jnp.float32).astype(jnp.bfloat16)
            return 0
        lax.fori_loop(0, D // dt, tile, 0)

    def add(j, s, slot):
        def some(i, _):
            a = pl.ds(pl.multiple_of(s * c + i * 16, 16), 16)
            b = pl.ds(pl.multiple_of(slot * c + i * 16, 16), 16)
            part[j, a, :] = (
                part[j, a, :].astype(jnp.float32) + rr[j, b, :].astype(jnp.float32)
            ).astype(jnp.bfloat16)
            return 0
        lax.fori_loop(0, c // 16, some, 0)

    def rs_round(j, r):
        @pl.when(r <= t)
        def _():
            @pl.when(t < last)
            def _():
                rs_copy(j, r, False).wait_recv()
                add(j, r, r)

            @pl.when(r < t)
            def _():
                rs_copy(j, r, False).start()

        @pl.when(last - r >= t)
        def _():
            s = last - r

            @pl.when(t > 0)
            def _():
                rs_copy(j, s, True).wait_recv()
                add(j, s, s + 1)

            @pl.when(s > t)
            def _():
                rs_copy(j, s, True).start()

    def loop(lo, hi_, body):
        def run(k, _):
            body(k)
            return 0
        lax.fori_loop(lo, hi_, run, 0)

    def done_out(j):
        return pltpu.make_async_copy(part.at[j, rows(t), :], gn.at[j], cg.at[j])

    loop(0, last, lambda k: ag_round(0, k))
    next_own(0, last)
    for i in range(pieces):
        w_copy(i).wait()
    for j in range(J):
        for s in range(n_t):
            ga_copy(j, s).wait()

    for j in range(J):
        own_cols(j).start()
        make_dpre(j)
        more = j + 1 < J
        if more:
            ag_round(j + 1, 0)
        else:
            if j > 0:
                rs_round(j - 1, last)
                done_out(j - 1).start()
        make_parts(j)
        if more:
            def both(r, j=j):
                rs_round(j, r)
                ag_round(j + 1, r + 1)
            loop(0, last - 1, both)
            rs_round(j, last - 1)
            next_own(j + 1, last)
        else:
            loop(0, n_t, lambda r: rs_round(j, r))
            done_out(j).start()

    for j in range(J):
        own_cols(j).wait()
        own_dpre(j).wait()
        done_out(j).wait()
        for p in range(1, n_h):
            xd_copy(j, p, came_from(p)).wait_recv()
            xd_copy(j, p, hi).wait_send()

        def finish(s, j=j):
            for p in range(1, n_h):
                xn_copy(j, s, p, came_from(p)).wait_recv()
                xn_copy(j, s, p, hi).wait_send()

            @pl.when((s <= t) & (t < last))
            def _():
                ag_copy(j, s, True).wait_send()

            @pl.when((s >= t) & (t > 0))
            def _():
                ag_copy(j, s, False).wait_send()

            @pl.when(s > t)
            def _():
                rs_copy(j, s, True).wait_send()

            @pl.when(s < t)
            def _():
                rs_copy(j, s, False).wait_send()
        loop(0, n_t, finish)


def exchange(normed, w_in, grad_act):
    n_t, n_d = lax.axis_size("tensor"), lax.axis_size("dp")
    n_h = n_d // 2
    J = STAGES
    local, D = normed.shape
    F = w_in.shape[1]
    c = local // J
    tok = n_t * c
    bf = jnp.bfloat16
    dma = pltpu.SemaphoreType.DMA
    hbm = pl.BlockSpec(memory_space=pl.ANY)
    flops = 4 * J * tok * D * F
    return pl.pallas_call(
        functools.partial(kernel, n_t, n_h, J, c),
        out_shape=(
            jax.ShapeDtypeStruct((n_h, J, tok, D // n_h), bf),
            jax.ShapeDtypeStruct((n_h, J, tok, F), bf),
            jax.ShapeDtypeStruct((J, c, D), bf),
        ),
        in_specs=[hbm] * 3,
        out_specs=(hbm, hbm, hbm),
        scratch_shapes=[
            pltpu.VMEM((D, F), bf),
            pltpu.VMEM((J, tok, D), bf),
            pltpu.VMEM((J, tok, D), bf),
            pltpu.VMEM((J, tok + c, D), bf),
            pltpu.VMEM((J, tok, F), bf),
            dma((8,)), dma((J, n_t)), dma((J,)),
            dma((J, n_t)), dma((J, n_t)), dma((J, n_t)),
            dma((J, n_t, n_h)), dma((J, n_t, n_h)), dma((J, n_h)), dma((J, n_h)),
            dma((J, n_t)), dma((J, n_t)), dma((J, n_t)), dma((J, n_t)),
            dma((J,)), dma((J,)), dma((J,)),
        ],
        cost_estimate=pl.CostEstimate(
            flops=flops, bytes_accessed=2 * D * F, transcendentals=J * tok * F),
        compiler_params=pltpu.CompilerParams(
            collective_id=0, has_side_effects=True, vmem_limit_bytes=64 * 1024 * 1024 - 131072),
    )(normed.reshape(J, c, D), w_in, grad_act.reshape(n_t, J, c, F))


def on_device(inputs, gain, w_in, grad_act, residual_gradient):
    values = inputs.astype(jnp.float32)
    centered_input = values - jnp.mean(values, axis=1, keepdims=True)
    inverse_deviation = lax.rsqrt(
        jnp.mean(centered_input * centered_input, axis=1, keepdims=True) + 1e-06
    )
    standardized_input = centered_input * inverse_deviation
    normed_output = (standardized_input * gain).astype(jnp.bfloat16)
    replicas = lax.axis_size("dp")
    ng, gd, gn = exchange(normed_output, w_in, grad_act)

    normed_gradient = gn.reshape(inputs.shape).astype(jnp.float32)
    scale_terms = jnp.sum(normed_gradient * standardized_input, axis=0)
    scale_gradient = lax.psum(scale_terms, ("dp", "tensor")) / replicas
    scaled_gradient = normed_gradient * gain
    first_average = jnp.mean(scaled_gradient, axis=1, keepdims=True)
    second_average = jnp.mean(scaled_gradient * standardized_input, axis=1, keepdims=True)
    block_input_gradient = (
        residual_gradient.astype(jnp.float32)
        + inverse_deviation
        * (scaled_gradient - first_average - standardized_input * second_average)
    ).astype(jnp.bfloat16)

    core = lax.rem(lax.axis_index("dp"), 2)
    cols = ng.reshape(-1, ng.shape[-1])
    dpre = gd.reshape(-1, gd.shape[-1])
    half = cols.shape[1] // 2
    theirs = lax.dynamic_slice_in_dim(cols, (1 - core) * half, half, 1)
    mine = lax.dynamic_slice_in_dim(cols, core * half, half, 1)
    sent = contract_rows(theirs, dpre).astype(jnp.bfloat16)
    got = lax.ppermute(sent, "dp", [(i, i ^ 1) for i in range(replicas)])
    grad_w = (contract_rows(mine, dpre) + got.astype(jnp.float32)) / replicas
    return (block_input_gradient, grad_w, scale_gradient)


def solution(mesh):
    return jax.shard_map(
        on_device,
        mesh=mesh,
        in_specs=(
            P(("dp", "tensor"), None),
            P(),
            P(None, "tensor"),
            P("dp", "tensor"),
            P(("dp", "tensor"), None),
        ),
        out_specs=(P(("dp", "tensor"), None), P("dp", "tensor"), P()),
        check_vma=False,
    )
```

```python
import functools

import jax
import jax.numpy as jnp
from jax import lax
from jax.experimental import pallas as pl
from jax.experimental.pallas import tpu as pltpu
from jax.sharding import PartitionSpec as P

MESH = pl.DeviceIdType.MESH
MOST_STAGES = 4


def contract_rows(left, right):
    return lax.dot_general(
        left, right, (((0,), (0,)), ((), ())), preferred_element_type=jnp.float32
    )


def gelu_slope(v):
    c = 0.7978845608028654
    vv = v * v
    th = jnp.tanh(c * v * (1.0 + 0.044715 * vv))
    return 0.5 * (1.0 + th) + 0.5 * v * (1.0 - th * th) * (c * (1.0 + 0.134145 * vv))


def kernel(
    n_t, n_h, J, c,
    nrm, w, ga, ng, gd, gn,
    w_v, ag, part, rr, dp,
    ld_w, ld_ga, ld_n,
    ag_recv, ag_send_r, ag_send_l,
    xn_send, xn_recv, xd_send, xd_recv, xf_send, xf_recv,
    rs_recv_r, rs_recv_l, rs_send_r, rs_send_l,
    cn, cd, cg,
):
    t = lax.axis_index("tensor")
    d = lax.axis_index("dp")
    hi, core = d // 2, lax.rem(d, 2)
    D, F = w_v.shape
    W = D // n_h
    last = n_t - 1

    def rows(s):
        return pl.ds(pl.multiple_of(s * c, c), c)

    square = n_h == 4
    direct = (1, 2) if square else tuple(range(1, n_h))

    def peer(p):
        if square:
            x, y = lax.rem(hi, 2), hi // 2
            return (1 - y if p >= 2 else y) * 2 + (1 - x if p % 2 else x)
        return lax.rem(hi + p, n_h)

    def came_from(p):
        return peer(p) if square else lax.rem(hi - p + n_h, n_h)

    def step(right):
        return {"tensor": lax.rem(t + 1, n_t) if right else lax.rem(t + last, n_t)}

    def ag_copy(j, s, right):
        block = ag.at[j, rows(s), :]
        sems = ag_send_r if right else ag_send_l
        return pltpu.make_async_remote_copy(
            block, block, sems.at[j, s], ag_recv.at[j, s],
            device_id=step(right), device_id_type=MESH)

    def rs_copy(j, s, right):
        slot = s + 1 if right else s
        send, recv = (rs_send_r, rs_recv_l) if right else (rs_send_l, rs_recv_r)
        return pltpu.make_async_remote_copy(
            part.at[j, rows(s), :], rr.at[j, rows(slot), :], send.at[j, s], recv.at[j, s],
            device_id=step(right), device_id_type=MESH)

    def xn_copy(j, s, p, whose):
        cols = pl.ds(pl.multiple_of(peer(p) * W, W), W)
        return pltpu.make_async_remote_copy(
            ag.at[j, rows(s), cols], ng.at[whose, j, rows(s), :],
            xn_send.at[j, s, p], xn_recv.at[j, s, p],
            device_id={"dp": peer(p) * 2 + core}, device_id_type=MESH)

    def xd_copy(j, p, whose):
        return pltpu.make_async_remote_copy(
            dp.at[j], gd.at[whose, j], xd_send.at[j, p], xd_recv.at[j, p],
            device_id={"dp": peer(p) * 2 + core}, device_id_type=MESH)

    def pass_copy(j, q, whose):
        part_rows = pl.ds((q - 1) * (n_t * c // 2), n_t * c // 2)
        block = gd.at[whose, j, part_rows, :]
        return pltpu.make_async_remote_copy(
            block, block, xf_send.at[j, q], xf_recv.at[j, q],
            device_id={"dp": peer(3 - q) * 2 + core}, device_id_type=MESH)

    def pass_on(j):
        if square:
            for q in (1, 2):
                xd_copy(j, q, peer(q)).wait_recv()
                pass_copy(j, q, peer(q)).start()

    def own_cols(j):
        return pltpu.make_async_copy(
            ag.at[j, :, pl.ds(pl.multiple_of(hi * W, W), W)], ng.at[hi, j], cn.at[j])

    def own_dpre(j):
        return pltpu.make_async_copy(dp.at[j], gd.at[hi, j], cd.at[j])

    pieces = ld_w.shape[0]
    depth = D // pieces

    def w_copy(i):
        r = pl.ds(i * depth, depth)
        return pltpu.make_async_copy(w.at[r, :], w_v.at[r, :], ld_w.at[i])

    def n_copy(j):
        return pltpu.make_async_copy(nrm.at[j], ag.at[j, rows(t), :], ld_n.at[j])

    def ga_copy(j, s):
        return pltpu.make_async_copy(ga.at[s, j], dp.at[j, pl.ds(s * c, c), :], ld_ga.at[j, s])

    for j in range(J):
        n_copy(j).start()
    barrier = pltpu.get_barrier_semaphore()
    for right in (True, False):
        @pl.when(t < last if right else t > 0)
        def _():
            pl.semaphore_signal(barrier, inc=1, device_id=step(right), device_id_type=MESH)
    for p in range(1, n_h):
        pl.semaphore_signal(barrier, inc=1, device_id={"dp": peer(p) * 2 + core}, device_id_type=MESH)
    pl.semaphore_wait(barrier, n_h - 1 + jnp.minimum(t, 1) + jnp.minimum(last - t, 1))
    for j in range(J):
        n_copy(j).wait()

    def send_own(j, right):
        @pl.when(t < last if right else t > 0)
        def _():
            ag_copy(j, t, right).start()

    def spread(j, s):
        for p in range(1, n_h):
            xn_copy(j, s, p, hi).start()

    send_own(0, True)
    send_own(0, False)
    for i in range(pieces):
        w_copy(i).start()
    for j in range(J):
        for s in range(n_t):
            ga_copy(j, s).start()
    for j in range(J):
        spread(j, t)

    def next_own(j, k):
        @pl.when((k == t) & (j + 1 < J))
        def _():
            send_own(j + 1, True)

        @pl.when((k == last - t) & (j + 1 < J))
        def _():
            send_own(j + 1, False)

    def ag_round(j, k):
        next_own(j, k)

        @pl.when(k < t)
        def _():
            s = t - 1 - k
            ag_copy(j, s, True).wait_recv()

            @pl.when(t < last)
            def _():
                ag_copy(j, s, True).start()
            spread(j, s)

        @pl.when(k < last - t)
        def _():
            s = t + 1 + k
            ag_copy(j, s, False).wait_recv()

            @pl.when(t > 0)
            def _():
                ag_copy(j, s, False).start()
            spread(j, s)

    def make_dpre(j):
        ft = 512 if F % 512 == 0 else 256

        def tile(i, _):
            cols = pl.ds(pl.multiple_of(i * ft, ft), ft)
            pre = jnp.dot(ag[j], w_v[:, cols], preferred_element_type=jnp.float32)
            g = dp[j, :, cols].astype(jnp.float32)
            dp[j, :, cols] = (g * gelu_slope(pre)).astype(jnp.bfloat16)
            return 0
        lax.fori_loop(0, F // ft, tile, 0)
        for p in direct:
            xd_copy(j, p, hi).start()
        own_dpre(j).start()

    def make_parts(j, lo, hi_):
        dt = 256

        def tile(i, _):
            cols = pl.ds(pl.multiple_of(i * dt, dt), dt)
            part[j, :, cols] = lax.dot_general(
                dp[j], w_v[cols, :], (((1,), (1,)), ((), ())),
                preferred_element_type=jnp.float32).astype(jnp.bfloat16)
            return 0
        lax.fori_loop(lo * (D // dt) // 2, hi_ * (D // dt) // 2, tile, 0)

    def add(j, s, slot):
        def some(i, _):
            a = pl.ds(pl.multiple_of(s * c + i * 16, 16), 16)
            b = pl.ds(pl.multiple_of(slot * c + i * 16, 16), 16)
            part[j, a, :] = (
                part[j, a, :].astype(jnp.float32) + rr[j, b, :].astype(jnp.float32)
            ).astype(jnp.bfloat16)
            return 0
        lax.fori_loop(0, c // 16, some, 0)

    def rs_round(j, r):
        @pl.when(r >= last - t)
        def _():
            s = r - (last - t)

            @pl.when(t < last)
            def _():
                rs_copy(j, s, False).wait_recv()
                add(j, s, s)

            @pl.when(s < t)
            def _():
                rs_copy(j, s, False).start()

        @pl.when(r >= t)
        def _():
            s = last - (r - t)

            @pl.when(t > 0)
            def _():
                rs_copy(j, s, True).wait_recv()
                add(j, s, s + 1)

            @pl.when(s > t)
            def _():
                rs_copy(j, s, True).start()

    def loop(lo, hi_, body):
        def run(k, _):
            body(k)
            return 0
        lax.fori_loop(lo, hi_, run, 0)

    def done_out(j):
        return pltpu.make_async_copy(part.at[j, rows(t), :], gn.at[j], cg.at[j])

    loop(0, last, lambda k: ag_round(0, k))
    next_own(0, last)
    for i in range(pieces):
        w_copy(i).wait()
    for j in range(J):
        for s in range(n_t):
            ga_copy(j, s).wait()

    a, b, e = n_t // 4, n_t // 2, 3 * n_t // 4

    def stage(j, reduce, gather):
        def steps(lo, hi_):
            def run(k):
                if reduce:
                    rs_round(j - 1, k)
                if gather:
                    @pl.when(k < last)
                    def _():
                        ag_round(j + 1, k)
            loop(lo, hi_, run)

        own_cols(j).start()
        steps(0, a)
        make_dpre(j)
        steps(a, b)
        make_parts(j, 0, 1)
        steps(b, e)
        if reduce:
            pass_on(j - 1)
        make_parts(j, 1, 2)
        steps(e, n_t)
        if reduce:
            done_out(j - 1).start()

    stage(0, False, True)
    loop(1, J - 1, lambda j: stage(j, True, True))
    stage(J - 1, True, False)
    loop(0, last, lambda r: rs_round(J - 1, r))
    pass_on(J - 1)
    rs_round(J - 1, last)
    done_out(J - 1).start()

    def end(j):
        own_cols(j).wait()
        own_dpre(j).wait()
        done_out(j).wait()
        for p in direct:
            if not square:
                xd_copy(j, p, came_from(p)).wait_recv()
            xd_copy(j, p, hi).wait_send()
        if square:
            for q in (1, 2):
                pass_copy(j, q, peer(3)).wait_recv()
                pass_copy(j, q, peer(q)).wait_send()

        def finish(s):
            for p in range(1, n_h):
                xn_copy(j, s, p, came_from(p)).wait_recv()
                xn_copy(j, s, p, hi).wait_send()

            @pl.when((s <= t) & (t < last))
            def _():
                ag_copy(j, s, True).wait_send()

            @pl.when((s >= t) & (t > 0))
            def _():
                ag_copy(j, s, False).wait_send()

            @pl.when(s > t)
            def _():
                rs_copy(j, s, True).wait_send()

            @pl.when(s < t)
            def _():
                rs_copy(j, s, False).wait_send()
        loop(0, n_t, finish)
    loop(0, J, end)


def sum_kernel(n_t, n_d, x, out, line, plane, send_t, recv_t, send_d, recv_d):
    t = lax.axis_index("tensor")
    d = lax.axis_index("dp")
    barrier = pltpu.get_barrier_semaphore()
    for p in range(1, n_t):
        pl.semaphore_signal(
            barrier, inc=1, device_id={"tensor": lax.rem(t + p, n_t)}, device_id_type=MESH)
    for p in range(1, n_d):
        pl.semaphore_signal(
            barrier, inc=1, device_id={"dp": lax.rem(d + p, n_d)}, device_id_type=MESH)
    pl.semaphore_wait(barrier, n_t + n_d - 2)

    def add_up(axis, me, n, buf, value, send, recv):
        buf[me] = value

        def copy(p, whose):
            return pltpu.make_async_remote_copy(
                buf.at[me], buf.at[whose], send.at[p], recv.at[p],
                device_id={axis: lax.rem(me + p, n)}, device_id_type=MESH)
        for p in range(1, n):
            copy(p, me).start()
        for p in range(1, n):
            copy(p, lax.rem(me - p + n, n)).wait_recv()
        total = buf[0]
        for i in range(1, n):
            total = total + buf[i]
        for p in range(1, n):
            copy(p, me).wait_send()
        return total

    total = add_up("tensor", t, n_t, line, x[...], send_t, recv_t)
    out[...] = add_up("dp", d, n_d, plane, total, send_d, recv_d)


def sum_everywhere(x):
    n_t, n_d = lax.axis_size("tensor"), lax.axis_size("dp")
    shape = (x.size // 128, 128)
    dma = pltpu.SemaphoreType.DMA
    vmem = pl.BlockSpec(memory_space=pltpu.VMEM)
    return pl.pallas_call(
        functools.partial(sum_kernel, n_t, n_d),
        out_shape=jax.ShapeDtypeStruct(shape, jnp.float32),
        in_specs=[vmem],
        out_specs=vmem,
        scratch_shapes=[
            pltpu.VMEM((n_t, *shape), jnp.float32),
            pltpu.VMEM((n_d, *shape), jnp.float32),
            dma((n_t,)), dma((n_t,)), dma((n_d,)), dma((n_d,)),
        ],
        compiler_params=pltpu.CompilerParams(collective_id=1, has_side_effects=True),
    )(x.reshape(shape)).reshape(x.shape)


def exchange(normed, w_in, grad_act):
    n_t, n_d = lax.axis_size("tensor"), lax.axis_size("dp")
    n_h = n_d // 2
    local, D = normed.shape
    J = min(MOST_STAGES, local // 16)
    F = w_in.shape[1]
    c = local // J
    tok = n_t * c
    bf = jnp.bfloat16
    dma = pltpu.SemaphoreType.DMA
    hbm = pl.BlockSpec(memory_space=pl.ANY)
    flops = 4 * J * tok * D * F
    return pl.pallas_call(
        functools.partial(kernel, n_t, n_h, J, c),
        out_shape=(
            jax.ShapeDtypeStruct((n_h, J, tok, D // n_h), bf),
            jax.ShapeDtypeStruct((n_h, J, tok, F), bf),
            jax.ShapeDtypeStruct((J, c, D), bf),
        ),
        in_specs=[hbm] * 3,
        out_specs=(hbm, hbm, hbm),
        scratch_shapes=[
            pltpu.VMEM((D, F), bf),
            pltpu.VMEM((J, tok, D), bf),
            pltpu.VMEM((J, tok, D), bf),
            pltpu.VMEM((J, tok + c, D), bf),
            pltpu.VMEM((J, tok, F), bf),
            dma((8,)), dma((J, n_t)), dma((J,)),
            dma((J, n_t)), dma((J, n_t)), dma((J, n_t)),
            dma((J, n_t, n_h)), dma((J, n_t, n_h)), dma((J, n_h)), dma((J, n_h)), dma((J, 3)), dma((J, 3)),
            dma((J, n_t)), dma((J, n_t)), dma((J, n_t)), dma((J, n_t)),
            dma((J,)), dma((J,)), dma((J,)),
        ],
        cost_estimate=pl.CostEstimate(
            flops=flops, bytes_accessed=2 * D * F, transcendentals=J * tok * F),
        compiler_params=pltpu.CompilerParams(
            collective_id=0, has_side_effects=True, vmem_limit_bytes=64 * 1024 * 1024 - 131072),
    )(normed.reshape(J, c, D), w_in, grad_act.reshape(n_t, J, c, F))


def on_device(inputs, gain, w_in, grad_act, residual_gradient):
    values = inputs.astype(jnp.float32)
    centered_input = values - jnp.mean(values, axis=1, keepdims=True)
    inverse_deviation = lax.rsqrt(
        jnp.mean(centered_input * centered_input, axis=1, keepdims=True) + 1e-06
    )
    standardized_input = centered_input * inverse_deviation
    normed_output = (standardized_input * gain).astype(jnp.bfloat16)
    replicas = lax.axis_size("dp")
    ng, gd, gn = exchange(normed_output, w_in, grad_act)

    normed_gradient = gn.reshape(inputs.shape).astype(jnp.float32)
    scale_terms = jnp.sum(normed_gradient * standardized_input, axis=0)
    scale_gradient = sum_everywhere(scale_terms) / replicas
    scaled_gradient = normed_gradient * gain
    first_average = jnp.mean(scaled_gradient, axis=1, keepdims=True)
    second_average = jnp.mean(scaled_gradient * standardized_input, axis=1, keepdims=True)
    block_input_gradient = (
        residual_gradient.astype(jnp.float32)
        + inverse_deviation
        * (scaled_gradient - first_average - standardized_input * second_average)
    ).astype(jnp.bfloat16)

    core = lax.rem(lax.axis_index("dp"), 2)
    cols = ng.reshape(-1, ng.shape[-1])
    dpre = gd.reshape(-1, gd.shape[-1])
    half = cols.shape[1] // 2
    theirs = lax.dynamic_slice_in_dim(cols, (1 - core) * half, half, 1)
    mine = lax.dynamic_slice_in_dim(cols, core * half, half, 1)
    sent = contract_rows(theirs, dpre).astype(jnp.bfloat16)
    got = lax.ppermute(sent, "dp", [(i, i ^ 1) for i in range(replicas)])
    grad_w = (contract_rows(mine, dpre) + got.astype(jnp.float32)) / replicas
    return (block_input_gradient, grad_w, scale_gradient)


def solution(mesh):
    return jax.shard_map(
        on_device,
        mesh=mesh,
        in_specs=(
            P(("dp", "tensor"), None),
            P(),
            P(None, "tensor"),
            P("dp", "tensor"),
            P(("dp", "tensor"), None),
        ),
        out_specs=(P(("dp", "tensor"), None), P("dp", "tensor"), P()),
        check_vma=False,
    )
```

```python
import functools

import jax
import jax.numpy as jnp
from jax import lax
from jax.experimental import pallas as pl
from jax.experimental.pallas import tpu as pltpu
from jax.sharding import PartitionSpec as P

MESH = pl.DeviceIdType.MESH
MOST_STAGES = 4


def contract_rows(left, right):
    return lax.dot_general(
        left, right, (((0,), (0,)), ((), ())), preferred_element_type=jnp.float32
    )


def gelu_slope(v):
    c = 0.7978845608028654
    vv = v * v
    th = jnp.tanh(c * v * (1.0 + 0.044715 * vv))
    return 0.5 * (1.0 + th) + 0.5 * v * (1.0 - th * th) * (c * (1.0 + 0.134145 * vv))


def kernel(
    n_t, n_h, J, c,
    nrm, w, ga, ng, gd, gn,
    w_v, ag, part, rr, dp,
    ld_w, ld_ga, ld_n,
    ag_recv, ag_send_r, ag_send_l,
    xn_send, xn_recv, xd_send, xd_recv, xf_send, xf_recv,
    rs_recv_r, rs_recv_l, rs_send_r, rs_send_l,
    cn, cd, cg,
):
    t = lax.axis_index("tensor")
    d = lax.axis_index("dp")
    hi, core = d // 2, lax.rem(d, 2)
    D, F = w_v.shape
    W = D // n_h
    last = n_t - 1

    def rows(s):
        return pl.ds(pl.multiple_of(s * c, c), c)

    square = n_h == 4
    direct = (1, 2) if square else tuple(range(1, n_h))

    def peer(p):
        if square:
            x, y = lax.rem(hi, 2), hi // 2
            return (1 - y if p >= 2 else y) * 2 + (1 - x if p % 2 else x)
        return lax.rem(hi + p, n_h)

    def came_from(p):
        return peer(p) if square else lax.rem(hi - p + n_h, n_h)

    def step(right):
        return {"tensor": lax.rem(t + 1, n_t) if right else lax.rem(t + last, n_t)}

    def ag_copy(j, s, right):
        block = ag.at[j, rows(s), :]
        sems = ag_send_r if right else ag_send_l
        return pltpu.make_async_remote_copy(
            block, block, sems.at[j, s], ag_recv.at[j, s],
            device_id=step(right), device_id_type=MESH)

    def rs_copy(j, s, right):
        slot = s + 1 if right else s
        send, recv = (rs_send_r, rs_recv_l) if right else (rs_send_l, rs_recv_r)
        return pltpu.make_async_remote_copy(
            part.at[j, rows(s), :], rr.at[j, rows(slot), :], send.at[j, s], recv.at[j, s],
            device_id=step(right), device_id_type=MESH)

    def xn_copy(j, s, p, whose):
        cols = pl.ds(pl.multiple_of(peer(p) * W, W), W)
        return pltpu.make_async_remote_copy(
            ag.at[j, rows(s), cols], ng.at[whose, j, rows(s), :],
            xn_send.at[j, s, p], xn_recv.at[j, s, p],
            device_id={"dp": peer(p) * 2 + core}, device_id_type=MESH)

    halves = 2 if square else 1

    def half_cols(h):
        return pl.ds(h * (F // halves), F // halves)

    def xd_copy(j, p, h, whose):
        return pltpu.make_async_remote_copy(
            dp.at[j, :, half_cols(h)], gd.at[whose, j, :, half_cols(h)],
            xd_send.at[j, p * halves + h], xd_recv.at[j, p * halves + h],
            device_id={"dp": peer(p) * 2 + core}, device_id_type=MESH)

    def pass_copy(j, q, whose):
        block = gd.at[whose, j, :, half_cols(q - 1)]
        return pltpu.make_async_remote_copy(
            block, block, xf_send.at[j, q], xf_recv.at[j, q],
            device_id={"dp": peer(3 - q) * 2 + core}, device_id_type=MESH)

    def pass_on(j):
        if square:
            for q in (1, 2):
                xd_copy(j, q, q - 1, peer(q)).wait_recv()
                pass_copy(j, q, peer(q)).start()

    def own_cols(j):
        return pltpu.make_async_copy(
            ag.at[j, :, pl.ds(pl.multiple_of(hi * W, W), W)], ng.at[hi, j], cn.at[j])

    def own_dpre(j):
        return pltpu.make_async_copy(dp.at[j], gd.at[hi, j], cd.at[j])

    pieces = ld_w.shape[0]
    depth = D // pieces

    def w_copy(i):
        r = pl.ds(i * depth, depth)
        return pltpu.make_async_copy(w.at[r, :], w_v.at[r, :], ld_w.at[i])

    def n_copy(j):
        return pltpu.make_async_copy(nrm.at[j], ag.at[j, rows(t), :], ld_n.at[j])

    def ga_copy(j, s):
        return pltpu.make_async_copy(ga.at[s, j], dp.at[j, pl.ds(s * c, c), :], ld_ga.at[j, s])

    for j in range(J):
        n_copy(j).start()
    barrier = pltpu.get_barrier_semaphore()
    for right in (True, False):
        @pl.when(t < last if right else t > 0)
        def _():
            pl.semaphore_signal(barrier, inc=1, device_id=step(right), device_id_type=MESH)
    for p in range(1, n_h):
        pl.semaphore_signal(barrier, inc=1, device_id={"dp": peer(p) * 2 + core}, device_id_type=MESH)
    pl.semaphore_wait(barrier, n_h - 1 + jnp.minimum(t, 1) + jnp.minimum(last - t, 1))
    for j in range(J):
        n_copy(j).wait()

    def send_own(j, right):
        @pl.when(t < last if right else t > 0)
        def _():
            ag_copy(j, t, right).start()

    def spread(j, s):
        for p in range(1, n_h):
            xn_copy(j, s, p, hi).start()

    send_own(0, True)
    send_own(0, False)
    for i in range(pieces):
        w_copy(i).start()
    for j in range(J):
        for s in range(n_t):
            ga_copy(j, s).start()
    for j in range(J):
        spread(j, t)

    def next_own(j, k):
        @pl.when((k == t) & (j + 1 < J))
        def _():
            send_own(j + 1, True)

        @pl.when((k == last - t) & (j + 1 < J))
        def _():
            send_own(j + 1, False)

    def ag_round(j, k):
        next_own(j, k)

        @pl.when(k < t)
        def _():
            s = t - 1 - k
            ag_copy(j, s, True).wait_recv()

            @pl.when(t < last)
            def _():
                ag_copy(j, s, True).start()
            spread(j, s)

        @pl.when(k < last - t)
        def _():
            s = t + 1 + k
            ag_copy(j, s, False).wait_recv()

            @pl.when(t > 0)
            def _():
                ag_copy(j, s, False).start()
            spread(j, s)

    def make_dpre(j):
        ft = 512 if F % 512 == 0 else 256

        def tile(i, _):
            cols = pl.ds(pl.multiple_of(i * ft, ft), ft)
            pre = jnp.dot(ag[j], w_v[:, cols], preferred_element_type=jnp.float32)
            g = dp[j, :, cols].astype(jnp.float32)
            dp[j, :, cols] = (g * gelu_slope(pre)).astype(jnp.bfloat16)
            return 0
        for h in range(halves):
            lax.fori_loop(h * (F // ft) // halves, (h + 1) * (F // ft) // halves, tile, 0)
            for p in direct:
                xd_copy(j, p, h, hi).start()
        own_dpre(j).start()

    def make_parts(j, lo, hi_):
        dt = 256

        def tile(i, _):
            cols = pl.ds(pl.multiple_of(i * dt, dt), dt)
            part[j, :, cols] = lax.dot_general(
                dp[j], w_v[cols, :], (((1,), (1,)), ((), ())),
                preferred_element_type=jnp.float32).astype(jnp.bfloat16)
            return 0
        lax.fori_loop(lo * (D // dt) // 2, hi_ * (D // dt) // 2, tile, 0)

    def add(j, s, slot):
        def some(i, _):
            a = pl.ds(pl.multiple_of(s * c + i * 16, 16), 16)
            b = pl.ds(pl.multiple_of(slot * c + i * 16, 16), 16)
            part[j, a, :] = (
                part[j, a, :].astype(jnp.float32) + rr[j, b, :].astype(jnp.float32)
            ).astype(jnp.bfloat16)
            return 0
        lax.fori_loop(0, c // 16, some, 0)

    def rs_round(j, r):
        @pl.when(r >= last - t)
        def _():
            s = r - (last - t)

            @pl.when(t < last)
            def _():
                rs_copy(j, s, False).wait_recv()
                add(j, s, s)

            @pl.when(s < t)
            def _():
                rs_copy(j, s, False).start()

        @pl.when(r >= t)
        def _():
            s = last - (r - t)

            @pl.when(t > 0)
            def _():
                rs_copy(j, s, True).wait_recv()
                add(j, s, s + 1)

            @pl.when(s > t)
            def _():
                rs_copy(j, s, True).start()

    def loop(lo, hi_, body):
        def run(k, _):
            body(k)
            return 0
        lax.fori_loop(lo, hi_, run, 0)

    def done_out(j):
        return pltpu.make_async_copy(part.at[j, rows(t), :], gn.at[j], cg.at[j])

    loop(0, last, lambda k: ag_round(0, k))
    next_own(0, last)
    for i in range(pieces):
        w_copy(i).wait()
    for j in range(J):
        for s in range(n_t):
            ga_copy(j, s).wait()

    a, b, e = n_t // 4, n_t // 2, 3 * n_t // 4

    def stage(j, reduce, gather):
        def steps(lo, hi_):
            def run(k):
                if reduce:
                    rs_round(j - 1, k)
                if gather:
                    @pl.when(k < last)
                    def _():
                        ag_round(j + 1, k)
            loop(lo, hi_, run)

        own_cols(j).start()
        steps(0, a)
        make_dpre(j)
        steps(a, b)
        make_parts(j, 0, 1)
        steps(b, e)
        if reduce:
            pass_on(j - 1)
        make_parts(j, 1, 2)
        steps(e, n_t)
        if reduce:
            done_out(j - 1).start()

    stage(0, False, True)
    loop(1, J - 1, lambda j: stage(j, True, True))
    stage(J - 1, True, False)
    loop(0, b, lambda r: rs_round(J - 1, r))
    pass_on(J - 1)
    loop(b, n_t, lambda r: rs_round(J - 1, r))
    done_out(J - 1).start()

    def end(j):
        own_cols(j).wait()
        own_dpre(j).wait()
        done_out(j).wait()
        for p in direct:
            for h in range(halves):
                if not (square and h == p - 1):
                    xd_copy(j, p, h, came_from(p)).wait_recv()
                xd_copy(j, p, h, hi).wait_send()
        if square:
            for q in (1, 2):
                pass_copy(j, q, peer(3)).wait_recv()
                pass_copy(j, q, peer(q)).wait_send()

        def finish(s):
            for p in range(1, n_h):
                xn_copy(j, s, p, came_from(p)).wait_recv()
                xn_copy(j, s, p, hi).wait_send()

            @pl.when((s <= t) & (t < last))
            def _():
                ag_copy(j, s, True).wait_send()

            @pl.when((s >= t) & (t > 0))
            def _():
                ag_copy(j, s, False).wait_send()

            @pl.when(s > t)
            def _():
                rs_copy(j, s, True).wait_send()

            @pl.when(s < t)
            def _():
                rs_copy(j, s, False).wait_send()
        loop(0, n_t, finish)
    loop(0, J, end)


def sum_kernel(n_t, n_d, x, out, line, plane, send_t, recv_t, send_d, recv_d):
    t = lax.axis_index("tensor")
    d = lax.axis_index("dp")
    barrier = pltpu.get_barrier_semaphore()
    for p in range(1, n_t):
        pl.semaphore_signal(
            barrier, inc=1, device_id={"tensor": lax.rem(t + p, n_t)}, device_id_type=MESH)
    for p in range(1, n_d):
        pl.semaphore_signal(
            barrier, inc=1, device_id={"dp": lax.rem(d + p, n_d)}, device_id_type=MESH)
    pl.semaphore_wait(barrier, n_t + n_d - 2)

    def add_up(axis, me, n, buf, value, send, recv):
        buf[me] = value

        def copy(p, whose):
            return pltpu.make_async_remote_copy(
                buf.at[me], buf.at[whose], send.at[p], recv.at[p],
                device_id={axis: lax.rem(me + p, n)}, device_id_type=MESH)
        for p in range(1, n):
            copy(p, me).start()
        for p in range(1, n):
            copy(p, lax.rem(me - p + n, n)).wait_recv()
        total = buf[0]
        for i in range(1, n):
            total = total + buf[i]
        for p in range(1, n):
            copy(p, me).wait_send()
        return total

    total = add_up("tensor", t, n_t, line, x[...], send_t, recv_t)
    out[...] = add_up("dp", d, n_d, plane, total, send_d, recv_d)


def sum_everywhere(x):
    n_t, n_d = lax.axis_size("tensor"), lax.axis_size("dp")
    shape = (x.size // 128, 128)
    dma = pltpu.SemaphoreType.DMA
    vmem = pl.BlockSpec(memory_space=pltpu.VMEM)
    return pl.pallas_call(
        functools.partial(sum_kernel, n_t, n_d),
        out_shape=jax.ShapeDtypeStruct(shape, jnp.float32),
        in_specs=[vmem],
        out_specs=vmem,
        scratch_shapes=[
            pltpu.VMEM((n_t, *shape), jnp.float32),
            pltpu.VMEM((n_d, *shape), jnp.float32),
            dma((n_t,)), dma((n_t,)), dma((n_d,)), dma((n_d,)),
        ],
        compiler_params=pltpu.CompilerParams(collective_id=1, has_side_effects=True),
    )(x.reshape(shape)).reshape(x.shape)


def exchange(normed, w_in, grad_act):
    n_t, n_d = lax.axis_size("tensor"), lax.axis_size("dp")
    n_h = n_d // 2
    local, D = normed.shape
    J = min(MOST_STAGES, local // 16)
    F = w_in.shape[1]
    c = local // J
    tok = n_t * c
    bf = jnp.bfloat16
    dma = pltpu.SemaphoreType.DMA
    hbm = pl.BlockSpec(memory_space=pl.ANY)
    flops = 4 * J * tok * D * F
    return pl.pallas_call(
        functools.partial(kernel, n_t, n_h, J, c),
        out_shape=(
            jax.ShapeDtypeStruct((n_h, J, tok, D // n_h), bf),
            jax.ShapeDtypeStruct((n_h, J, tok, F), bf),
            jax.ShapeDtypeStruct((J, c, D), bf),
        ),
        in_specs=[hbm] * 3,
        out_specs=(hbm, hbm, hbm),
        scratch_shapes=[
            pltpu.VMEM((D, F), bf),
            pltpu.VMEM((J, tok, D), bf),
            pltpu.VMEM((J, tok, D), bf),
            pltpu.VMEM((J, tok + c, D), bf),
            pltpu.VMEM((J, tok, F), bf),
            dma((8,)), dma((J, n_t)), dma((J,)),
            dma((J, n_t)), dma((J, n_t)), dma((J, n_t)),
            dma((J, n_t, n_h)), dma((J, n_t, n_h)), dma((J, 2 * n_h)), dma((J, 2 * n_h)), dma((J, 3)), dma((J, 3)),
            dma((J, n_t)), dma((J, n_t)), dma((J, n_t)), dma((J, n_t)),
            dma((J,)), dma((J,)), dma((J,)),
        ],
        cost_estimate=pl.CostEstimate(
            flops=flops, bytes_accessed=2 * D * F, transcendentals=J * tok * F),
        compiler_params=pltpu.CompilerParams(
            collective_id=0, has_side_effects=True, vmem_limit_bytes=64 * 1024 * 1024 - 131072),
    )(normed.reshape(J, c, D), w_in, grad_act.reshape(n_t, J, c, F))


def on_device(inputs, gain, w_in, grad_act, residual_gradient):
    values = inputs.astype(jnp.float32)
    centered_input = values - jnp.mean(values, axis=1, keepdims=True)
    inverse_deviation = lax.rsqrt(
        jnp.mean(centered_input * centered_input, axis=1, keepdims=True) + 1e-06
    )
    standardized_input = centered_input * inverse_deviation
    normed_output = (standardized_input * gain).astype(jnp.bfloat16)
    replicas = lax.axis_size("dp")
    ng, gd, gn = exchange(normed_output, w_in, grad_act)

    normed_gradient = gn.reshape(inputs.shape).astype(jnp.float32)
    scale_terms = jnp.sum(normed_gradient * standardized_input, axis=0)
    scale_gradient = sum_everywhere(scale_terms) / replicas
    scaled_gradient = normed_gradient * gain
    first_average = jnp.mean(scaled_gradient, axis=1, keepdims=True)
    second_average = jnp.mean(scaled_gradient * standardized_input, axis=1, keepdims=True)
    block_input_gradient = (
        residual_gradient.astype(jnp.float32)
        + inverse_deviation
        * (scaled_gradient - first_average - standardized_input * second_average)
    ).astype(jnp.bfloat16)

    core = lax.rem(lax.axis_index("dp"), 2)
    cols = ng.reshape(-1, ng.shape[-1])
    dpre = gd.reshape(-1, gd.shape[-1])
    half = cols.shape[1] // 2
    theirs = lax.dynamic_slice_in_dim(cols, (1 - core) * half, half, 1)
    mine = lax.dynamic_slice_in_dim(cols, core * half, half, 1)
    sent = contract_rows(theirs, dpre).astype(jnp.bfloat16)
    got = lax.ppermute(sent, "dp", [(i, i ^ 1) for i in range(replicas)])
    grad_w = (contract_rows(mine, dpre) + got.astype(jnp.float32)) / replicas
    return (block_input_gradient, grad_w, scale_gradient)


def solution(mesh):
    return jax.shard_map(
        on_device,
        mesh=mesh,
        in_specs=(
            P(("dp", "tensor"), None),
            P(),
            P(None, "tensor"),
            P("dp", "tensor"),
            P(("dp", "tensor"), None),
        ),
        out_specs=(P(("dp", "tensor"), None), P("dp", "tensor"), P()),
        check_vma=False,
    )
```
